256 devices in a mesh: grp: 16 (over y, x_lo, core), slab: 16 (over z, x_hi).
Axes of the slice: x: 4 (x_hi: 2, x_lo: 2; x = x_hi * 2 + x_lo), y: 4, z: 8, core: 2. Of those that a mesh axis runs over, the one named last changes fastest.
Arguments:
- basis_atom_masses: bfloat16 [3, 256, 128, 128], P(None, 'slab'), may hold values from 0.03 to 34
- right_dual_factors: float32 [16, 3, 256, 128, 128], P('grp', None, 'slab'), may hold values from 0.03 to 34
- observed_mass_snapshot: float32 [16, 256, 128, 128], P('grp', 'slab'), may hold values from 0.03 to 34
- mixing_coefficient_tags: int32 [16, 3], P('grp'), may hold values from 1 to 16
Outputs:
- barycenter: float32 [16, 256, 128, 128], P('grp', 'slab')
- new_scalings: float32 [16, 3, 256, 128, 128], P('grp', None, 'slab')
- atom_gradient: float32 [3, 256, 128, 128], P(None, 'grp', 'slab')
The draws below stay inside these ranges and needn't reach their ends.
All inputs are finite; a program needn't handle non-finite values.
Results may differ from the reference program's by a relative error of at most 0.0003.
Values may be sent and summed in bfloat16 or wider, within the bound.
A program may use at most 64 MiB of HBM per device.

```python
import math
import jax
import jax.numpy as jnp
from jax import lax

NX = 256
NY = 128
NZ = 128
ATOMS = 3
REACH = 4
GROUPS = 16


def profiled(key, leading, spread, jitter):
    subkeys = jax.random.split(key, 4)
    along_x = jax.random.uniform(subkeys[0], leading + (NX, 1, 1), jnp.float32, -spread, spread)
    along_y = jax.random.uniform(subkeys[1], leading + (1, NY, 1), jnp.float32, -spread, spread)
    along_z = jax.random.uniform(subkeys[2], leading + (1, 1, NZ), jnp.float32, -spread, spread)
    texture = jax.random.uniform(subkeys[3], leading + (NX, NY, NZ), jnp.float32, -jitter, jitter)
    return jnp.exp(along_x + along_y + along_z + texture)


def draw_basis_atom_masses(key, part):
    key = jax.random.fold_in(key, 11)
    values = profiled(key, (ATOMS,), 0.8, 0.4)
    return values.astype(jnp.bfloat16)


def draw_right_dual_factors(key, part):
    key = jax.random.fold_in(key, 23)
    values = profiled(key, (GROUPS, ATOMS), 0.8, 0.4)
    return values.astype(jnp.float32)


def draw_observed_mass_snapshot(key, part):
    key = jax.random.fold_in(key, 37)
    values = profiled(key, (GROUPS,), 0.8, 0.4)
    return values.astype(jnp.float32)


def touch_ends(entries, key, least, high):
    shape = entries.shape
    place = [jax.random.randint(jax.random.fold_in(key, axis), (), 0, shape[axis]) for axis in range(len(shape))]
    entries = entries.at[tuple(place)].set(least)
    longest = shape.index(max(shape))
    place[longest] = (place[longest] + 1) % shape[longest]
    return entries.at[tuple(place)].set(high)


def setup_inputs(seed: int = 0) -> dict:
    arg_keys = jax.random.split(jax.random.key(seed), 5)
    return {
        "basis_atom_masses": draw_basis_atom_masses(jax.random.fold_in(arg_keys[4], 71), 0),
        "right_dual_factors": draw_right_dual_factors(jax.random.fold_in(arg_keys[4], 71), 0),
        "observed_mass_snapshot": draw_observed_mass_snapshot(jax.random.fold_in(arg_keys[4], 71), 0),
        "mixing_coefficient_tags": touch_ends(jax.random.randint(arg_keys[3], (GROUPS, ATOMS), 1, 17), jax.random.fold_in(arg_keys[3], 1), 1, 16).astype(jnp.int32),
    }


sharpness = 3.0

def profile(offset):
    values = jnp.exp(-sharpness * (offset / REACH) ** 2) / (REACH * math.sqrt(math.pi / sharpness))
    return jnp.where(jnp.abs(offset) <= REACH, values, jnp.zeros_like(values))

def gaussian(count):
    positions = jnp.arange(count)
    offset = (positions[:, None] - positions[None, :]).astype(jnp.float32)
    return profile(offset)

def heat_blur(values, abscissa_axis, ordinate_axis, height_axis):
    highest = lax.Precision.HIGHEST
    values = jnp.einsum('axyz,zw->axyw', values, height_axis, precision=highest)
    values = jnp.einsum('axyz,yw->axwz', values, ordinate_axis, precision=highest)
    return jnp.einsum('axyz,xw->awyz', values, abscissa_axis, precision=highest)

def reference(basis_atom_masses, right_dual_factors, observed_mass_snapshot, mixing_coefficient_tags):
    abscissa_axis = gaussian(NX)
    ordinate_axis = gaussian(NY)
    height_axis = gaussian(NZ)
    dictionary = basis_atom_masses.astype(jnp.float32)

    def lone_cohort_case(running_total, cohort_arguments):
        right_dual_factor, goal_mass, coefficient_line = cohort_arguments
        blend = coefficient_line.astype(jnp.float32) / jnp.sum(coefficient_line).astype(jnp.float32)
        blend = blend[:, None, None, None]
        blurred_right_factor = heat_blur(right_dual_factor, abscissa_axis, ordinate_axis, height_axis)
        first_scale = dictionary / blurred_right_factor
        kern_u = heat_blur(first_scale, abscissa_axis, ordinate_axis, height_axis)
        barycenter = jnp.exp(lax.optimization_barrier(jnp.sum(blend * jnp.log(kern_u), axis=0)))
        new_scaling = barycenter[None] / kern_u
        pulled = blend * ((barycenter - goal_mass) * barycenter)[None] / kern_u
        sensitivity_mass = heat_blur(pulled, abscissa_axis, ordinate_axis, height_axis) / blurred_right_factor
        return (running_total + sensitivity_mass, (barycenter, new_scaling))
    initial_slot = jnp.zeros(dictionary.shape, jnp.float32)
    sensitivity_mass, returned_tuple = lax.scan(lone_cohort_case, initial_slot, (right_dual_factors, observed_mass_snapshot, mixing_coefficient_tags))
    return (returned_tuple[0], returned_tuple[1], sensitivity_mass)
```

```python
import math

import jax
import jax.numpy as jnp
import ml_dtypes
import numpy as np
from jax import lax
from jax.experimental import pallas as pl
from jax.experimental.pallas import tpu as pltpu
from jax.sharding import PartitionSpec as P

REACH = 4
SHARPNESS = 3.0
ATOMS = 3
ROWS = 16
NY = 128
NZ = 128
HALF = 8
MESH = pl.DeviceIdType.MESH
f32 = jnp.float32
bf16 = jnp.bfloat16

TAPS = [math.exp(-SHARPNESS * (d / REACH) ** 2) / (REACH * math.sqrt(math.pi / SHARPNESS)) for d in range(REACH + 1)]

V_LOW, V_HIGH = math.log(0.0295), math.log(34.6)
F_LOW, F_HIGH = math.log(8.0e-4), math.log(5.2e3)


def code_of(low, high):
    scale = 65532.0 / (high - low)
    return scale, -32766.0 - low * scale


V_CODE = code_of(V_LOW, V_HIGH)
F_CODE = code_of(F_LOW, F_HIGH)


def encode(values, code):
    scale, shift = code
    return jnp.floor(jnp.log(values) * scale + (shift + 0.5)).astype(jnp.int32).astype(jnp.int16)


def decode(codes, code):
    scale, shift = code
    return jnp.exp(codes.astype(jnp.int32).astype(f32) * (1.0 / scale) - shift / scale)


def band(n):
    i = np.arange(n)
    offset = np.abs(i[:, None] - i[None, :])
    taps = np.array(TAPS, np.float32)
    return np.where(offset <= REACH, taps[np.minimum(offset, REACH)], np.float32(0))


def band_parts(n):
    g = band(n)
    high = g.astype(ml_dtypes.bfloat16)
    low = (g - high.astype(np.float32)).astype(ml_dtypes.bfloat16)
    return high, low


def matrices():
    high, low = band_parts(NZ)
    zero = np.zeros_like(low)
    along_z = np.block([[high, low], [high, zero]])
    high, low = band_parts(NY)
    zero = np.zeros_like(low)
    along_y = np.block([[high, high], [low, zero]])
    return along_z.astype(ml_dtypes.bfloat16), along_y.astype(ml_dtypes.bfloat16)


def parts(x):
    high = x.astype(bf16)
    return high, (x - high.astype(f32)).astype(bf16)


def kernel(
    v_hbm, b_hbm, p_hbm, tags, gz, gy,
    bary_hbm, scal_hbm, grad_hbm,
    vbuf, fbuf, rk, lk, bbuf, pbuf, bary, scal,
    s1, s2, s3, r1, r2, r3,
    gsend, crecv, ysum, yrecv, fsend, frecv, gout,
    in_sem, out_sem, h_send, h_recv, c_send, c_recv, y_send, y_recv, f_send, f_recv,
):
    g = lax.axis_index("grp")
    s = lax.axis_index("slab")
    y, lo, c = g // 4, (g // 2) % 2, g % 2
    left = (g, (s + 15) % 16)
    right = (g, (s + 1) % 16)
    twin = (y * 4 + lo * 2 + (1 - c), s)

    def across_y(d):
        return (((y + d) % 4) * 4 + lo * 2 + c, s)

    def owner(i):
        return (s, 4 * y + (1 - c) + 2 * i)

    def giver(l):
        return ((s // 4) * 4 + l * 2 + (1 - s % 2), g)

    v_in = [pltpu.make_async_copy(v_hbm.at[0, a], vbuf.at[a, pl.ds(REACH, ROWS)], in_sem.at[a]) for a in range(ATOMS)]
    p_in = pltpu.make_async_copy(p_hbm, pbuf, in_sem.at[3])
    b_in = pltpu.make_async_copy(b_hbm.at[0], bbuf, in_sem.at[4])
    for copy in v_in + [p_in, b_in]:
        copy.start()

    barrier = pltpu.get_barrier_semaphore()
    peers = [left, right, twin] + [across_y(d) for d in (1, 2, 3)] + [owner(0), owner(1), giver(0), giver(1)]
    for peer in peers:
        pl.semaphore_signal(barrier, inc=1, device_id=peer, device_id_type=MESH)
    pl.semaphore_wait(barrier, len(peers))

    has_left = (s > 0).astype(f32)
    has_right = (s < 15).astype(f32)

    def remote(src, dst, send, recv, device):
        return pltpu.make_async_remote_copy(src_ref=src, dst_ref=dst, send_sem=send, recv_sem=recv, device_id=device, device_id_type=MESH)

    def halos(stage, a):
        src, dst = ((s1, r1), (s2, r2), (s3, r3))[stage]
        return [
            remote(src.at[a, pl.ds(0, 4)], dst.at[a, 0], h_send.at[stage, a, 0], h_recv.at[stage, a, 0], right),
            remote(src.at[a, pl.ds(4, 4)], dst.at[a, 1], h_send.at[stage, a, 1], h_recv.at[stage, a, 1], left),
        ]

    def blur(buf, a, r):
        x = TAPS[0] * buf[a, r + REACH]
        for d in range(1, REACH + 1):
            x = x + TAPS[d] * (buf[a, r + REACH - d] + buf[a, r + REACH + d])
        high, low = parts(x)
        t = jnp.dot(jnp.concatenate([high, low], 1), gz[...], preferred_element_type=f32)
        high, low = parts(t[:, :NZ] + t[:, NZ:])
        t = jnp.dot(gy[...], jnp.concatenate([high, low], 0), preferred_element_type=f32)
        return t[:NY] + t[NY:]

    def row(part, i):
        return (4 + i) if part == 0 else (12 + i) % 16

    for a in range(ATOMS):
        v_in[a].wait()

        @pl.loop(0, HALF, unroll=2)
        def _(i):
            s1[a, i] = encode(vbuf[a, row(1, i) + REACH], V_CODE)

        for copy in halos(0, a):
            copy.start()

    p_in.wait()

    def first(a, part):
        @pl.loop(0, HALF, unroll=4)
        def _(i):
            r = row(part, i)
            k = 1.0 / blur(vbuf, a, r)
            rk[a, r] = k
            f = pbuf[a, r].astype(f32) * k
            fbuf[a, r + REACH] = f
            if part == 1:
                s2[a, i] = encode(f, F_CODE)

    def second(a, part):
        @pl.loop(0, HALF, unroll=4)
        def _(i):
            r = row(part, i)
            lk[a, r] = jnp.log(blur(fbuf, a, r))

    def land(stage, a, buf):
        for copy in halos(stage, a):
            copy.wait_recv()
        dst = (r1, r2, r3)[stage]

        def value(x):
            return x.astype(f32) if stage == 2 else decode(x, (V_CODE, F_CODE)[stage])

        @pl.loop(0, 4, unroll=2)
        def _(i):
            buf[a, i] = value(dst[a, 0, i]) * has_left
            buf[a, i + REACH + ROWS] = value(dst[a, 1, i]) * has_right

    for a in range(ATOMS):
        first(a, 0)
    for a in range(ATOMS):
        land(0, a, vbuf)
        first(a, 1)
        for copy in halos(1, a):
            copy.start()
        second(a, 0)

    total = jnp.zeros((8, NZ), f32)
    weights = []
    for a in range(ATOMS):
        weights.append(jnp.full((8, NZ), tags[0, a], jnp.int32).astype(f32))
        total = total + weights[a]
    blend = [(w / total)[:1] for w in weights]

    def middle(part):
        @pl.loop(0, HALF, unroll=2)
        def _(i):
            r = row(part, i)
            logs = [lk[a, r] for a in range(ATOMS)]
            mean = blend[0] * logs[0] + blend[1] * logs[1] + blend[2] * logs[2]
            center = jnp.exp(mean)
            bary[r] = center
            miss = center - bbuf[r]
            for a in range(ATOMS):
                ratio = jnp.exp(mean - logs[a])
                scal[a, r] = ratio
                pulled = blend[a] * miss * ratio
                vbuf[a, r + REACH] = pulled
                if part == 1:
                    s3[a, i] = pulled.astype(bf16)

    b_in.wait()
    land(1, 0, fbuf)
    second(0, 1)
    land(1, 1, fbuf)
    second(1, 1)
    middle(0)
    land(1, 2, fbuf)
    second(2, 1)
    middle(1)
    for a in range(ATOMS):
        for copy in halos(2, a):
            copy.start()
    results = [pltpu.make_async_copy(bary, bary_hbm.at[0], out_sem.at[0]), pltpu.make_async_copy(scal, scal_hbm.at[0], out_sem.at[1])]
    for copy in results:
        copy.start()

    def to_twin(a, part):
        return remote(gsend.at[a, part, c], crecv.at[a, part], c_send.at[a, part], c_recv.at[a, part], twin)

    def to_y(a, part, d):
        there = (y + d) % 4
        return remote(
            ysum.at[a, part, pl.ds(2 * there, 2)], yrecv.at[a, part, d - 1], y_send.at[a, part, d - 1], y_recv.at[a, part, d - 1], across_y(d)
        )

    def to_owner(a, part, i):
        return remote(fsend.at[a, part, i], frecv.at[a, part, lo], f_send.at[a, part, i], f_recv.at[a, part, lo], owner(i))

    def third(a, part):
        @pl.loop(0, HALF, unroll=4)
        def _(i):
            r = row(part, i)
            t = (blur(vbuf, a, r) * rk[a, r]).reshape(8, 2, 8, NZ)
            gsend[a, part, 0, :, i] = t[:, 0]
            gsend[a, part, 1, :, i] = t[:, 1]

        to_twin(a, part).start()

    def over_cores(a, part):
        to_twin(a, part).wait_recv()

        @pl.loop(0, 8, unroll=2)
        def _(j):
            ysum[a, part, j] = gsend[a, part, 1 - c, j] + crecv[a, part, j]

        for d in (2, 1, 3):
            to_y(a, part, d).start()

    def over_y(a, part):
        for d in (1, 3, 2):
            to_y(a, part, d).wait_recv()
        for i in range(2):
            t = ysum[a, part, 2 * y + i]
            for d in range(3):
                t = t + yrecv[a, part, d, i]
            fsend[a, part, i] = t
            to_owner(a, part, i).start()

    for a in range(ATOMS):
        third(a, 0)
    for a in range(ATOMS):
        over_cores(a, 0)
    land(2, 0, vbuf)
    third(0, 1)
    for a in range(ATOMS):
        over_y(a, 0)
    over_cores(0, 1)
    land(2, 1, vbuf)
    third(1, 1)
    over_y(0, 1)
    over_cores(1, 1)
    land(2, 2, vbuf)
    third(2, 1)
    over_y(1, 1)
    over_cores(2, 1)
    over_y(2, 1)

    for a in range(ATOMS):
        for part in range(2):
            for l in range(2):
                remote(fsend.at[a, part, 0], frecv.at[a, part, l], f_send.at[a, part, 0], f_recv.at[a, part, l], owner(0)).wait_recv()
            t = frecv[a, part, 0] + frecv[a, part, 1]
            if part == 0:
                gout[a, pl.ds(4, 8)] = t
            else:
                gout[a, pl.ds(12, 4)] = t[:4]
                gout[a, pl.ds(0, 4)] = t[4:]
    last = pltpu.make_async_copy(gout, grad_hbm, out_sem.at[2])
    last.start()

    for a in range(ATOMS):
        for stage in range(3):
            for copy in halos(stage, a):
                copy.wait_send()
        for part in range(2):
            to_twin(a, part).wait_send()
            for d in (1, 2, 3):
                to_y(a, part, d).wait_send()
            for i in range(2):
                to_owner(a, part, i).wait_send()
    for copy in results:
        copy.wait()
    last.wait()


def local(basis_atom_masses, right_dual_factors, observed_mass_snapshot, mixing_coefficient_tags):
    gz, gy = matrices()
    plane = (NY, NZ)
    vmem = pltpu.VMEM
    dma = pltpu.SemaphoreType.DMA
    anywhere = pl.BlockSpec(memory_space=pl.ANY)
    return pl.pallas_call(
        kernel,
        out_shape=(
            jax.ShapeDtypeStruct((1, ROWS) + plane, f32),
            jax.ShapeDtypeStruct((1, ATOMS, ROWS) + plane, f32),
            jax.ShapeDtypeStruct((ATOMS, ROWS, 8, NZ), f32),
        ),
        in_specs=[
            anywhere,
            anywhere,
            anywhere,
            pl.BlockSpec(memory_space=pltpu.SMEM),
            pl.BlockSpec(memory_space=vmem),
            pl.BlockSpec(memory_space=vmem),
        ],
        out_specs=(anywhere, anywhere, anywhere),
        scratch_shapes=[
            vmem((ATOMS, ROWS + 2 * REACH) + plane, f32),
            vmem((ATOMS, ROWS + 2 * REACH) + plane, f32),
            vmem((ATOMS, ROWS) + plane, f32),
            vmem((ATOMS, ROWS) + plane, f32),
            vmem((ROWS,) + plane, f32),
            vmem((ATOMS, ROWS) + plane, bf16),
            vmem((ROWS,) + plane, f32),
            vmem((ATOMS, ROWS) + plane, f32),
            vmem((ATOMS, HALF) + plane, jnp.int16),
            vmem((ATOMS, HALF) + plane, jnp.int16),
            vmem((ATOMS, HALF) + plane, bf16),
            vmem((ATOMS, 2, 4) + plane, jnp.int16),
            vmem((ATOMS, 2, 4) + plane, jnp.int16),
            vmem((ATOMS, 2, 4) + plane, bf16),
            vmem((ATOMS, 2, 2, 8, HALF, 8, NZ), f32),
            vmem((ATOMS, 2, 8, HALF, 8, NZ), f32),
            vmem((ATOMS, 2, 8, HALF, 8, NZ), f32),
            vmem((ATOMS, 2, 3, 2, HALF, 8, NZ), f32),
            vmem((ATOMS, 2, 2, HALF, 8, NZ), f32),
            vmem((ATOMS, 2, 2, HALF, 8, NZ), f32),
            vmem((ATOMS, ROWS, 8, NZ), f32),
            dma((5,)),
            dma((3,)),
            dma((3, ATOMS, 2)),
            dma((3, ATOMS, 2)),
            dma((ATOMS, 2)),
            dma((ATOMS, 2)),
            dma((ATOMS, 2, 3)),
            dma((ATOMS, 2, 3)),
            dma((ATOMS, 2, 2)),
            dma((ATOMS, 2, 2)),
        ],
        compiler_params=pltpu.CompilerParams(collective_id=0, has_side_effects=True, vmem_limit_bytes=60 * 2**20),
        name="sinkhorn_step",
    )(right_dual_factors, observed_mass_snapshot, basis_atom_masses, mixing_coefficient_tags, gz, gy)


def solution(mesh):
    placed = (
        P(None, "slab", None, None),
        P("grp", None, "slab", None, None),
        P("grp", "slab", None, None),
        P("grp", None),
    )
    return jax.shard_map(
        local,
        mesh=mesh,
        in_specs=placed,
        out_specs=(
            P("grp", "slab", None, None),
            P("grp", None, "slab", None, None),
            P(None, "grp", "slab", None),
        ),
        check_vma=False,
    )
```

```python
import math

import jax
import jax.numpy as jnp
import ml_dtypes
import numpy as np
from jax import lax
from jax.experimental import pallas as pl
from jax.experimental.pallas import tpu as pltpu
from jax.sharding import PartitionSpec as P

REACH = 4
SHARPNESS = 3.0
ATOMS = 3
ROWS = 16
NY = 128
NZ = 128
HALF = 8
MESH = pl.DeviceIdType.MESH
f32 = jnp.float32
bf16 = jnp.bfloat16
LN2 = math.log(2.0)
CODE_TOP = 32760.0
VMEM_LIMIT = 61184 * 2**10

TAPS = [math.exp(-SHARPNESS * (d / REACH) ** 2) / (REACH * math.sqrt(math.pi / SHARPNESS)) for d in range(REACH + 1)]

V_LOW, V_HIGH = math.log(0.0295), math.log(34.6)
F_LOW, F_HIGH = math.log(8.0e-4), math.log(5.2e3)


def code_of(low, high):
    scale = 65532.0 / (high - low)
    return scale, -32766.0 - low * scale


V_CODE = code_of(V_LOW, V_HIGH)
F_CODE = code_of(F_LOW, F_HIGH)


def encode(values, code):
    scale, shift = code
    return jnp.floor(jnp.log(values) * scale + (shift + 0.5)).astype(jnp.int32).astype(jnp.int16)


def decode(codes, code):
    scale, shift = code
    return jnp.exp(codes.astype(jnp.int32).astype(f32) * (1.0 / scale) - shift / scale)


HIGH = [float(np.float32(t).astype(ml_dtypes.bfloat16)) for t in TAPS]
LOW = [float((np.float32(t) - np.float32(h)).astype(ml_dtypes.bfloat16)) for t, h in zip(TAPS, HIGH)]


def band(taps, n):
    offset = jnp.abs(lax.broadcasted_iota(jnp.int32, (n, n), 0) - lax.broadcasted_iota(jnp.int32, (n, n), 1))
    g = jnp.zeros((n, n), f32)
    for d, tap in enumerate(taps):
        g = jnp.where(offset == d, tap, g)
    return g.astype(bf16)


def parts(x):
    high = x.astype(bf16)
    return high, (x - high.astype(f32)).astype(bf16)


def kernel(
    v_hbm, b_hbm, p_hbm, tags,
    bary, scal, gout,
    gz, gy, vbuf, fbuf, rk, lk, bbuf, pbuf,
    s1, s2, s3, r1, r2, r3,
    gsend, crecv, ysum, ycode, yrecv, fsize, fsend0, fsend1, frecv0, frecv1,
    in_sem, h_send, h_recv, c_send, c_recv, y_send, y_recv, f_send, f_recv,
):
    g = lax.axis_index("grp")
    s = lax.axis_index("slab")
    y, lo, c = g // 4, (g // 2) % 2, g % 2
    left = (g, (s + 15) % 16)
    right = (g, (s + 1) % 16)
    twin = (y * 4 + lo * 2 + (1 - c), s)

    def across_y(d):
        return (((y + d) % 4) * 4 + lo * 2 + c, s)

    z = s // 2
    pair = (y + 2 * c) % 4

    def ahead(k, i):
        return (z + k + 4 * i) % 8

    def owner(i):
        return (s, 2 * ahead(pair, i) + 1 - c)

    giver_core = 1 - s % 2
    giver_y = ((s // 2 - g // 2 + 8) % 8 + 4 - 2 * giver_core) % 4

    def giver(l):
        return (giver_y * 4 + l * 2 + giver_core, g)

    v_in = [pltpu.make_async_copy(v_hbm.at[0, a], vbuf.at[a, pl.ds(REACH, ROWS)], in_sem.at[a]) for a in range(ATOMS)]
    p_in = pltpu.make_async_copy(p_hbm, pbuf, in_sem.at[3])
    b_in = pltpu.make_async_copy(b_hbm.at[0], bbuf, in_sem.at[4])
    for copy in v_in + [p_in, b_in]:
        copy.start()

    barrier = pltpu.get_barrier_semaphore()
    peers = [left, right, twin] + [across_y(d) for d in (1, 2, 3)] + [owner(0), owner(1), giver(0), giver(1)]
    for peer in peers:
        pl.semaphore_signal(barrier, inc=1, device_id=peer, device_id_type=MESH)

    high, low, zero = band(HIGH, NZ), band(LOW, NZ), jnp.zeros((NZ, NZ), bf16)
    gz[...] = jnp.concatenate([jnp.concatenate([high, low], 1), jnp.concatenate([high, zero], 1)], 0)
    gy[...] = jnp.concatenate([jnp.concatenate([high, high], 1), jnp.concatenate([low, zero], 1)], 0)

    has_left = (s > 0).astype(f32)
    has_right = (s < 15).astype(f32)

    def remote(src, dst, send, recv, device):
        return pltpu.make_async_remote_copy(src_ref=src, dst_ref=dst, send_sem=send, recv_sem=recv, device_id=device, device_id_type=MESH)

    def halos(stage, a):
        src, dst = ((s1, r1), (s2, r2), (s3, r3))[stage]
        return [
            remote(src.at[a, pl.ds(0, 4)], dst.at[a, 0], h_send.at[stage, a, 0], h_recv.at[stage, a, 0], right),
            remote(src.at[a, pl.ds(4, 4)], dst.at[a, 1], h_send.at[stage, a, 1], h_recv.at[stage, a, 1], left),
        ]

    def blur(buf, a, r):
        x = TAPS[0] * buf[a, r + REACH]
        for d in range(1, REACH + 1):
            x = x + TAPS[d] * (buf[a, r + REACH - d] + buf[a, r + REACH + d])
        high, low = parts(x)
        t = jnp.dot(jnp.concatenate([high, low], 1), gz[...], preferred_element_type=f32)
        high, low = parts(t[:, :NZ] + t[:, NZ:])
        t = jnp.dot(gy[...], jnp.concatenate([high, low], 0), preferred_element_type=f32)
        return t[:NY] + t[NY:]

    def row(part, i):
        return (4 + i) if part == 0 else (12 + i) % 16

    for a in range(ATOMS):
        v_in[a].wait()

        @pl.loop(0, HALF, unroll=2)
        def _(i):
            s1[a, i] = encode(vbuf[a, row(1, i) + REACH], V_CODE)

        if a == 0:
            pl.semaphore_wait(barrier, len(peers))
        for copy in halos(0, a):
            copy.start()

    p_in.wait()

    def first(a, part):
        @pl.loop(0, HALF, unroll=4)
        def _(i):
            r = row(part, i)
            k = 1.0 / blur(vbuf, a, r)
            rk[a, r] = k
            f = pbuf[a, r].astype(f32) * k
            fbuf[a, r + REACH] = f
            if part == 1:
                s2[a, i] = encode(f, F_CODE)

    def second(a, part):
        @pl.loop(0, HALF, unroll=4)
        def _(i):
            r = row(part, i)
            lk[a, r] = jnp.log(blur(fbuf, a, r))

    def land(stage, a, buf):
        for copy in halos(stage, a):
            copy.wait_recv()
        dst = (r1, r2, r3)[stage]

        def value(x):
            return x.astype(f32) if stage == 2 else decode(x, (V_CODE, F_CODE)[stage])

        @pl.loop(0, 4, unroll=2)
        def _(i):
            buf[a, i] = value(dst[a, 0, i]) * has_left
            buf[a, i + REACH + ROWS] = value(dst[a, 1, i]) * has_right

    for a in range(ATOMS):
        first(a, 0)
    for a in range(ATOMS):
        land(0, a, vbuf)
        first(a, 1)
        for copy in halos(1, a):
            copy.start()
        second(a, 0)

    total = jnp.zeros((8, NZ), f32)
    weights = []
    for a in range(ATOMS):
        weights.append(jnp.full((8, NZ), tags[0, a], jnp.int32).astype(f32))
        total = total + weights[a]
    blend = [(w / total)[:1] for w in weights]

    def middle(part):
        @pl.loop(0, HALF, unroll=2)
        def _(i):
            r = row(part, i)
            logs = [lk[a, r] for a in range(ATOMS)]
            mean = blend[0] * logs[0] + blend[1] * logs[1] + blend[2] * logs[2]
            center = jnp.exp(mean)
            bary[0, r] = center
            miss = center - bbuf[r]
            for a in range(ATOMS):
                ratio = jnp.exp(mean - logs[a])
                scal[0, a, r] = ratio
                pulled = blend[a] * miss * ratio
                vbuf[a, r + REACH] = pulled
                if part == 1:
                    s3[a, i] = pulled.astype(bf16)

    b_in.wait()
    land(1, 0, fbuf)
    second(0, 1)
    land(1, 1, fbuf)
    second(1, 1)
    middle(0)
    land(1, 2, fbuf)
    second(2, 1)
    middle(1)
    for a in range(ATOMS):
        for copy in halos(2, a):
            copy.start()

    def to_twin(a, part):
        return remote(gsend.at[a, part, c], crecv.at[a, part], c_send.at[a, part], c_recv.at[a, part], twin)

    def to_y(a, part, d):
        return remote(
            ycode.at[a, part, (pair + d) % 4], yrecv.at[a, part, d - 1], y_send.at[a, part, d - 1], y_recv.at[a, part, d - 1], across_y(d)
        )

    def to_owner(a, part, i):
        if part == 0:
            src, dst, n = fsend0.at[i], frecv0.at[lo], 0
        else:
            src, dst, n = fsend1.at[a, i], frecv1.at[a, lo], 1 + a
        return remote(src, dst, f_send.at[n, i], f_recv.at[n, lo], owner(i))

    def from_giver(a, part, l):
        if part == 0:
            src, dst, n = fsend0.at[0], frecv0.at[l], 0
        else:
            src, dst, n = fsend1.at[a, 0], frecv1.at[a, l], 1 + a
        return remote(src, dst, f_send.at[n, 0], f_recv.at[n, l], owner(0))

    def pack(t):
        top = jnp.maximum(jnp.max(jnp.abs(t), axis=0), 1e-30)
        size = jnp.ceil(jnp.log(top) * (16.0 / LN2))
        code = jnp.floor(t * (CODE_TOP * jnp.exp(size * (-LN2 / 16.0)))[None] + 0.5)
        return code.reshape(64, NZ).astype(jnp.int32).astype(jnp.int16), size

    def narrow(size):
        return size.astype(jnp.int32).astype(jnp.int16)

    def units(size):
        return jnp.exp(size.astype(jnp.int32).astype(f32) * (LN2 / 16.0)) * (1.0 / CODE_TOP)

    def unpack(code, unit):
        return code.astype(jnp.int32).astype(f32).reshape(HALF, 8, NZ) * unit[None]

    def third(a, part):
        @pl.loop(0, HALF, unroll=4)
        def _(i):
            r = row(part, i)
            t = (blur(vbuf, a, r) * rk[a, r]).reshape(8, 2, 8, NZ)
            gsend[a, part, 0, :, i] = t[:, 0]
            gsend[a, part, 1, :, i] = t[:, 1]

        to_twin(a, part).start()

    def over_cores(a, part):
        to_twin(a, part).wait_recv()

        @pl.loop(0, 4)
        def _(k):
            sizes = []
            for i in range(2):
                j = ahead(k, i)
                t = gsend[a, part, 1 - c, j] + crecv[a, part, j]
                ysum[a, part, k, i] = t
                ycode[a, part, k, pl.ds(64 * i, 64)], size = pack(t)
                sizes.append(size)
            ycode[a, part, k, pl.ds(128, 16)] = narrow(jnp.concatenate(sizes, 0))

        for d in (2, 1, 3):
            to_y(a, part, d).start()

    def over_y(a, part):
        for d in (1, 3, 2):
            to_y(a, part, d).wait_recv()
        scales = [units(yrecv[a, part, d, pl.ds(128, 16)]) for d in range(3)]
        for i in range(2):
            t = ysum[a, part, pair, i]
            for d in range(3):
                t = t + unpack(yrecv[a, part, d, pl.ds(64 * i, 64)], scales[d][8 * i : 8 * i + 8])
            code, size = pack(t)
            if part == 0:
                fsend0[i, pl.ds(64 * a, 64)] = code
                fsize[a, i] = size
                if a == ATOMS - 1:
                    sizes = jnp.concatenate([fsize[0, i], fsize[1, i], size, size], 0)
                    fsend0[i, pl.ds(192, 32)] = narrow(sizes)
                    to_owner(a, part, i).start()
            else:
                fsend1[a, i, pl.ds(0, 64)] = code
                fsend1[a, i, pl.ds(64, 16)] = narrow(jnp.concatenate([size, size], 0))
                to_owner(a, part, i).start()

    for a in range(ATOMS):
        third(a, 0)
    for a in range(ATOMS):
        over_cores(a, 0)
    land(2, 0, vbuf)
    third(0, 1)
    for a in range(ATOMS):
        over_y(a, 0)
    over_cores(0, 1)
    land(2, 1, vbuf)
    third(1, 1)
    over_y(0, 1)
    over_cores(1, 1)
    land(2, 2, vbuf)
    third(2, 1)
    over_y(1, 1)
    over_cores(2, 1)
    over_y(2, 1)

    for l in range(2):
        from_giver(0, 0, l).wait_recv()
    scales = [units(frecv0[l, pl.ds(192, 32)]) for l in range(2)]
    for a in range(ATOMS):
        t = [unpack(frecv0[l, pl.ds(64 * a, 64)], scales[l][8 * a : 8 * a + 8]) for l in range(2)]
        gout[a, pl.ds(4, 8)] = t[0] + t[1]
    for a in range(ATOMS):
        for l in range(2):
            from_giver(a, 1, l).wait_recv()
        t = [unpack(frecv1[a, l, pl.ds(0, 64)], units(frecv1[a, l, pl.ds(64, 16)])[:8]) for l in range(2)]
        t = t[0] + t[1]
        gout[a, pl.ds(12, 4)] = t[:4]
        gout[a, pl.ds(0, 4)] = t[4:]

    for a in range(ATOMS):
        for stage in range(3):
            for copy in halos(stage, a):
                copy.wait_send()
        for part in range(2):
            to_twin(a, part).wait_send()
            for d in (1, 2, 3):
                to_y(a, part, d).wait_send()
            for i in range(2 if part or a == 0 else 0):
                to_owner(a, part, i).wait_send()


def local(basis_atom_masses, right_dual_factors, observed_mass_snapshot, mixing_coefficient_tags):
    plane = (NY, NZ)
    vmem = pltpu.VMEM
    dma = pltpu.SemaphoreType.DMA
    outside = pl.BlockSpec(memory_space=pltpu.HBM)
    return pl.pallas_call(
        kernel,
        out_shape=(
            vmem((1, ROWS) + plane, f32),
            vmem((1, ATOMS, ROWS) + plane, f32),
            vmem((ATOMS, ROWS, 8, NZ), f32),
        ),
        in_specs=[
            outside,
            outside,
            outside,
            pl.BlockSpec(memory_space=pltpu.SMEM),
        ],
        out_specs=(pl.BlockSpec(memory_space=vmem),) * 3,
        scratch_shapes=[
            vmem((2 * NZ, 2 * NZ), bf16),
            vmem((2 * NY, 2 * NY), bf16),
            vmem((ATOMS, ROWS + 2 * REACH) + plane, f32),
            vmem((ATOMS, ROWS + 2 * REACH) + plane, f32),
            vmem((ATOMS, ROWS) + plane, f32),
            vmem((ATOMS, ROWS) + plane, f32),
            vmem((ROWS,) + plane, f32),
            vmem((ATOMS, ROWS) + plane, bf16),
            vmem((ATOMS, HALF) + plane, jnp.int16),
            vmem((ATOMS, HALF) + plane, jnp.int16),
            vmem((ATOMS, HALF) + plane, bf16),
            vmem((ATOMS, 2, 4) + plane, jnp.int16),
            vmem((ATOMS, 2, 4) + plane, jnp.int16),
            vmem((ATOMS, 2, 4) + plane, bf16),
            vmem((ATOMS, 2, 2, 8, HALF, 8, NZ), f32),
            vmem((ATOMS, 2, 8, HALF, 8, NZ), f32),
            vmem((ATOMS, 2, 4, 2, HALF, 8, NZ), f32),
            vmem((ATOMS, 2, 4, 144, NZ), jnp.int16),
            vmem((ATOMS, 2, 3, 144, NZ), jnp.int16),
            vmem((ATOMS, 2, 8, NZ), f32),
            vmem((2, 224, NZ), jnp.int16),
            vmem((ATOMS, 2, 80, NZ), jnp.int16),
            vmem((2, 224, NZ), jnp.int16),
            vmem((ATOMS, 2, 80, NZ), jnp.int16),
            dma((5,)),
            dma((3, ATOMS, 2)),
            dma((3, ATOMS, 2)),
            dma((ATOMS, 2)),
            dma((ATOMS, 2)),
            dma((ATOMS, 2, 3)),
            dma((ATOMS, 2, 3)),
            dma((1 + ATOMS, 2)),
            dma((1 + ATOMS, 2)),
        ],
        compiler_params=pltpu.CompilerParams(collective_id=0, has_side_effects=True, vmem_limit_bytes=VMEM_LIMIT),
        name="sinkhorn_step",
    )(right_dual_factors, observed_mass_snapshot, basis_atom_masses, mixing_coefficient_tags)


def solution(mesh):
    placed = (
        P(None, "slab", None, None),
        P("grp", None, "slab", None, None),
        P("grp", "slab", None, None),
        P("grp", None),
    )
    return jax.shard_map(
        local,
        mesh=mesh,
        in_specs=placed,
        out_specs=(
            P("grp", "slab", None, None),
            P("grp", None, "slab", None, None),
            P(None, "grp", "slab", None),
        ),
        check_vma=False,
    )
```

```python
import math

import jax
import jax.numpy as jnp
import ml_dtypes
import numpy as np
from jax import lax
from jax.experimental import pallas as pl
from jax.experimental.pallas import tpu as pltpu
from jax.sharding import PartitionSpec as P

REACH = 4
SHARPNESS = 3.0
ATOMS = 3
ROWS = 16
NY = 128
NZ = 128
HALF = 8
MESH = pl.DeviceIdType.MESH
f32 = jnp.float32
bf16 = jnp.bfloat16
LN2 = math.log(2.0)
CODE_TOP = 32760.0
VMEM_LIMIT = 61184 * 2**10

TAPS = [math.exp(-SHARPNESS * (d / REACH) ** 2) / (REACH * math.sqrt(math.pi / SHARPNESS)) for d in range(REACH + 1)]

V_LOW, V_HIGH = math.log(0.0295), math.log(34.6)
F_LOW, F_HIGH = math.log(8.0e-4), math.log(5.2e3)


def code_of(low, high):
    scale = 65532.0 / (high - low)
    return scale, -32766.0 - low * scale


V_CODE = code_of(V_LOW, V_HIGH)
F_CODE = code_of(F_LOW, F_HIGH)


def encode(values, code):
    scale, shift = code
    return jnp.floor(jnp.log(values) * scale + (shift + 0.5)).astype(jnp.int32).astype(jnp.int16)


def decode(codes, code):
    scale, shift = code
    return jnp.exp(codes.astype(jnp.int32).astype(f32) * (1.0 / scale) - shift / scale)


HIGH = [float(np.float32(t).astype(ml_dtypes.bfloat16)) for t in TAPS]
LOW = [float((np.float32(t) - np.float32(h)).astype(ml_dtypes.bfloat16)) for t, h in zip(TAPS, HIGH)]


def band(taps, n):
    offset = jnp.abs(lax.broadcasted_iota(jnp.int32, (n, n), 0) - lax.broadcasted_iota(jnp.int32, (n, n), 1))
    g = jnp.zeros((n, n), f32)
    for d, tap in enumerate(taps):
        g = jnp.where(offset == d, tap, g)
    return g.astype(bf16)


def parts(x):
    high = x.astype(bf16)
    return high, (x - high.astype(f32)).astype(bf16)


def kernel(
    v_hbm, b_hbm, p_hbm, tags,
    bary, scal, gout,
    gz, gy, vbuf, fbuf, rk, lk, bbuf, pbuf,
    s1, s2, s3, r1, r2, r3,
    gsend, crecv, ysum, ycode, yrecv, fsize, fsend0, fsend1, frecv0, frecv1,
    in_sem, h_send, h_recv, c_send, c_recv, y_send, y_recv, f_send, f_recv,
):
    g = lax.axis_index("grp")
    s = lax.axis_index("slab")
    y, lo, c = g // 4, (g // 2) % 2, g % 2
    left = (g, (s + 15) % 16)
    right = (g, (s + 1) % 16)
    twin = (y * 4 + lo * 2 + (1 - c), s)

    def across_y(d):
        return (((y + d) % 4) * 4 + lo * 2 + c, s)

    z = s // 2
    pair = (y + 2 * c) % 4

    def ahead(k, i):
        return (z + k + 4 * i) % 8

    def owner(i):
        return (s, 2 * ahead(pair, i) + 1 - c)

    giver_core = 1 - s % 2
    giver_y = ((s // 2 - g // 2 + 8) % 8 + 4 - 2 * giver_core) % 4

    def giver(l):
        return (giver_y * 4 + l * 2 + giver_core, g)

    v_in = [pltpu.make_async_copy(v_hbm.at[0, a], vbuf.at[a, pl.ds(REACH, ROWS)], in_sem.at[a]) for a in range(ATOMS)]
    p_in = pltpu.make_async_copy(p_hbm, pbuf, in_sem.at[3])
    b_in = pltpu.make_async_copy(b_hbm.at[0], bbuf, in_sem.at[4])
    for copy in v_in + [p_in, b_in]:
        copy.start()

    barrier = pltpu.get_barrier_semaphore()
    peers = [left, right, twin] + [across_y(d) for d in (1, 2, 3)] + [owner(0), owner(1), giver(0), giver(1)]
    for peer in peers:
        pl.semaphore_signal(barrier, inc=1, device_id=peer, device_id_type=MESH)

    high, low, zero = band(HIGH, NZ), band(LOW, NZ), jnp.zeros((NZ, NZ), bf16)
    gz[...] = jnp.concatenate([jnp.concatenate([high, low], 1), jnp.concatenate([high, zero], 1)], 0)
    gy[...] = jnp.concatenate([jnp.concatenate([high, high], 1), jnp.concatenate([low, zero], 1)], 0)

    has_left = (s > 0).astype(f32)
    has_right = (s < 15).astype(f32)

    def remote(src, dst, send, recv, device):
        return pltpu.make_async_remote_copy(src_ref=src, dst_ref=dst, send_sem=send, recv_sem=recv, device_id=device, device_id_type=MESH)

    def halo(stage, a, q):
        src, dst = ((s1, r1), (s2, r2), (s3, r3))[stage]
        return remote(
            src.at[a, pl.ds(4 * q, 4)], dst.at[a, q], h_send.at[stage, a, q], h_recv.at[stage, a, q], (right, left)[q]
        )

    def halos(stage, a):
        return [halo(stage, a, q) for q in range(2)]

    def blur(buf, a, r):
        x = TAPS[0] * buf[a, r + REACH]
        for d in range(1, REACH + 1):
            x = x + TAPS[d] * (buf[a, r + REACH - d] + buf[a, r + REACH + d])
        high, low = parts(x)
        t = jnp.dot(jnp.concatenate([high, low], 1), gz[...], preferred_element_type=f32)
        high, low = parts(t[:, :NZ] + t[:, NZ:])
        t = jnp.dot(gy[...], jnp.concatenate([high, low], 0), preferred_element_type=f32)
        return t[:NY] + t[NY:]

    def row(part, i):
        return (4 + i) if part == 0 else (12 + i) % 16

    for a in range(ATOMS):
        v_in[a].wait()

        @pl.loop(0, HALF, unroll=2)
        def _(i):
            s1[a, i] = encode(vbuf[a, row(1, i) + REACH], V_CODE)

        if a == 0:
            pl.semaphore_wait(barrier, len(peers))
        for copy in halos(0, a):
            copy.start()

    p_in.wait()

    def span(side):
        return (0, HALF) if side is None else (4 * side, 4 * side + 4)

    def first(a, part):
        @pl.loop(0, HALF, unroll=8 if part else 4)
        def _(i):
            r = row(part, i)
            k = 1.0 / blur(vbuf, a, r)
            rk[a, r] = k
            f = pbuf[a, r].astype(f32) * k
            fbuf[a, r + REACH] = f
            if part == 1:
                s2[a, i] = encode(f, F_CODE)

    def second(a, part, side=None):
        @pl.loop(*span(side), unroll=8 if part and side is None else 4)
        def _(i):
            r = row(part, i)
            lk[a, r] = jnp.log(blur(fbuf, a, r))

    def land(stage, a, buf, side=None):
        sides = (0, 1) if side is None else (side,)
        for q in sides:
            halo(stage, a, 1 - q).wait_recv()
        dst = (r1, r2, r3)[stage]

        def value(x):
            return x.astype(f32) if stage == 2 else decode(x, (V_CODE, F_CODE)[stage])

        @pl.loop(0, 4, unroll=4)
        def _(i):
            if 1 in sides:
                buf[a, i] = value(dst[a, 0, i]) * has_left
            if 0 in sides:
                buf[a, i + REACH + ROWS] = value(dst[a, 1, i]) * has_right

    for a in range(ATOMS):
        first(a, 0)
    for a in range(ATOMS):
        land(0, a, vbuf)
        first(a, 1)
        for copy in halos(1, a):
            copy.start()
        second(a, 0)

    total = jnp.zeros((8, NZ), f32)
    weights = []
    for a in range(ATOMS):
        weights.append(jnp.full((8, NZ), tags[0, a], jnp.int32).astype(f32))
        total = total + weights[a]
    blend = [(w / total)[:1] for w in weights]

    def middle(part, side=None):
        @pl.loop(*span(side), unroll=2)
        def _(i):
            r = row(part, i)
            logs = [lk[a, r] for a in range(ATOMS)]
            mean = blend[0] * logs[0] + blend[1] * logs[1] + blend[2] * logs[2]
            center = jnp.exp(mean)
            bary[0, r] = center
            miss = center - bbuf[r]
            for a in range(ATOMS):
                ratio = jnp.exp(mean - logs[a])
                scal[0, a, r] = ratio
                pulled = blend[a] * miss * ratio
                vbuf[a, r + REACH] = pulled
                if part == 1:
                    s3[a, i] = pulled.astype(bf16)

    b_in.wait()
    land(1, 0, fbuf)
    second(0, 1)
    land(1, 1, fbuf)
    second(1, 1)
    middle(0)
    for side in range(2):
        land(1, 2, fbuf, side)
        second(2, 1, side)
        middle(1, side)
        for a in range(ATOMS):
            halo(2, a, side).start()

    def to_twin(a, part):
        return remote(gsend.at[a, part, c], crecv.at[a, part], c_send.at[a, part], c_recv.at[a, part], twin)

    def to_y(a, part, d):
        return remote(
            ycode.at[a, part, (pair + d) % 4], yrecv.at[a, part, d - 1], y_send.at[a, part, d - 1], y_recv.at[a, part, d - 1], across_y(d)
        )

    def to_owner(a, part, i):
        if part == 0:
            src, dst, n = fsend0.at[i], frecv0.at[lo], 0
        else:
            src, dst, n = fsend1.at[a, i], frecv1.at[a, lo], 1 + a
        return remote(src, dst, f_send.at[n, i], f_recv.at[n, lo], owner(i))

    def from_giver(a, part, l):
        if part == 0:
            src, dst, n = fsend0.at[0], frecv0.at[l], 0
        else:
            src, dst, n = fsend1.at[a, 0], frecv1.at[a, l], 1 + a
        return remote(src, dst, f_send.at[n, 0], f_recv.at[n, l], owner(0))

    def pack(t):
        top = jnp.maximum(jnp.max(jnp.abs(t), axis=0), 1e-30)
        size = jnp.ceil(jnp.log(top) * (16.0 / LN2))
        code = jnp.floor(t * (CODE_TOP * jnp.exp(size * (-LN2 / 16.0)))[None] + 0.5)
        return code.reshape(64, NZ).astype(jnp.int32).astype(jnp.int16), size

    def narrow(size):
        return size.astype(jnp.int32).astype(jnp.int16)

    def units(size):
        return jnp.exp(size.astype(jnp.int32).astype(f32) * (LN2 / 16.0)) * (1.0 / CODE_TOP)

    def unpack(code, unit):
        return code.astype(jnp.int32).astype(f32).reshape(HALF, 8, NZ) * unit[None]

    def third(a, part):
        @pl.loop(0, HALF, unroll=8 if part else 4)
        def _(i):
            r = row(part, i)
            t = (blur(vbuf, a, r) * rk[a, r]).reshape(8, 2, 8, NZ)
            gsend[a, part, 0, :, i] = t[:, 0]
            gsend[a, part, 1, :, i] = t[:, 1]

        to_twin(a, part).start()

    def over_cores(a, part):
        to_twin(a, part).wait_recv()

        @pl.loop(0, 4, unroll=4)
        def _(k):
            sizes = []
            for i in range(2):
                j = ahead(k, i)
                t = gsend[a, part, 1 - c, j] + crecv[a, part, j]
                ysum[a, part, k, i] = t
                ycode[a, part, k, pl.ds(64 * i, 64)], size = pack(t)
                sizes.append(size)
            ycode[a, part, k, pl.ds(128, 16)] = narrow(jnp.concatenate(sizes, 0))

        for d in (2, 1, 3):
            to_y(a, part, d).start()

    def over_y(a, part):
        for d in (1, 3, 2):
            to_y(a, part, d).wait_recv()
        scales = [units(yrecv[a, part, d, pl.ds(128, 16)]) for d in range(3)]
        for i in range(2):
            t = ysum[a, part, pair, i]
            for d in range(3):
                t = t + unpack(yrecv[a, part, d, pl.ds(64 * i, 64)], scales[d][8 * i : 8 * i + 8])
            code, size = pack(t)
            if part == 0:
                fsend0[i, pl.ds(64 * a, 64)] = code
                fsize[a, i] = size
                if a == ATOMS - 1:
                    sizes = jnp.concatenate([fsize[0, i], fsize[1, i], size, size], 0)
                    fsend0[i, pl.ds(192, 32)] = narrow(sizes)
                    to_owner(a, part, i).start()
            else:
                fsend1[a, i, pl.ds(0, 64)] = code
                fsend1[a, i, pl.ds(64, 16)] = narrow(jnp.concatenate([size, size], 0))
                to_owner(a, part, i).start()

    for a in range(ATOMS):
        third(a, 0)
    for a in range(ATOMS):
        over_cores(a, 0)
    land(2, 0, vbuf)
    third(0, 1)
    for a in range(ATOMS):
        over_y(a, 0)
    over_cores(0, 1)
    land(2, 1, vbuf)
    third(1, 1)
    over_y(0, 1)
    over_cores(1, 1)
    land(2, 2, vbuf)
    third(2, 1)
    over_y(1, 1)
    over_cores(2, 1)
    over_y(2, 1)

    for l in range(2):
        from_giver(0, 0, l).wait_recv()
    scales = [units(frecv0[l, pl.ds(192, 32)]) for l in range(2)]
    for a in range(ATOMS):
        t = [unpack(frecv0[l, pl.ds(64 * a, 64)], scales[l][8 * a : 8 * a + 8]) for l in range(2)]
        gout[a, pl.ds(4, 8)] = t[0] + t[1]
    for a in range(ATOMS):
        for l in range(2):
            from_giver(a, 1, l).wait_recv()
        t = [unpack(frecv1[a, l, pl.ds(0, 64)], units(frecv1[a, l, pl.ds(64, 16)])[:8]) for l in range(2)]
        t = t[0] + t[1]
        gout[a, pl.ds(12, 4)] = t[:4]
        gout[a, pl.ds(0, 4)] = t[4:]

    for a in range(ATOMS):
        for stage in range(3):
            for copy in halos(stage, a):
                copy.wait_send()
        for part in range(2):
            to_twin(a, part).wait_send()
            for d in (1, 2, 3):
                to_y(a, part, d).wait_send()
            for i in range(2 if part or a == 0 else 0):
                to_owner(a, part, i).wait_send()


def local(basis_atom_masses, right_dual_factors, observed_mass_snapshot, mixing_coefficient_tags):
    plane = (NY, NZ)
    vmem = pltpu.VMEM
    dma = pltpu.SemaphoreType.DMA
    outside = pl.BlockSpec(memory_space=pltpu.HBM)
    return pl.pallas_call(
        kernel,
        out_shape=(
            vmem((1, ROWS) + plane, f32),
            vmem((1, ATOMS, ROWS) + plane, f32),
            vmem((ATOMS, ROWS, 8, NZ), f32),
        ),
        in_specs=[
            outside,
            outside,
            outside,
            pl.BlockSpec(memory_space=pltpu.SMEM),
        ],
        out_specs=(pl.BlockSpec(memory_space=vmem),) * 3,
        scratch_shapes=[
            vmem((2 * NZ, 2 * NZ), bf16),
            vmem((2 * NY, 2 * NY), bf16),
            vmem((ATOMS, ROWS + 2 * REACH) + plane, f32),
            vmem((ATOMS, ROWS + 2 * REACH) + plane, f32),
            vmem((ATOMS, ROWS) + plane, f32),
            vmem((ATOMS, ROWS) + plane, f32),
            vmem((ROWS,) + plane, f32),
            vmem((ATOMS, ROWS) + plane, bf16),
            vmem((ATOMS, HALF) + plane, jnp.int16),
            vmem((ATOMS, HALF) + plane, jnp.int16),
            vmem((ATOMS, HALF) + plane, bf16),
            vmem((ATOMS, 2, 4) + plane, jnp.int16),
            vmem((ATOMS, 2, 4) + plane, jnp.int16),
            vmem((ATOMS, 2, 4) + plane, bf16),
            vmem((ATOMS, 2, 2, 8, HALF, 8, NZ), f32),
            vmem((ATOMS, 2, 8, HALF, 8, NZ), f32),
            vmem((ATOMS, 2, 4, 2, HALF, 8, NZ), f32),
            vmem((ATOMS, 2, 4, 144, NZ), jnp.int16),
            vmem((ATOMS, 2, 3, 144, NZ), jnp.int16),
            vmem((ATOMS, 2, 8, NZ), f32),
            vmem((2, 224, NZ), jnp.int16),
            vmem((ATOMS, 2, 80, NZ), jnp.int16),
            vmem((2, 224, NZ), jnp.int16),
            vmem((ATOMS, 2, 80, NZ), jnp.int16),
            dma((5,)),
            dma((3, ATOMS, 2)),
            dma((3, ATOMS, 2)),
            dma((ATOMS, 2)),
            dma((ATOMS, 2)),
            dma((ATOMS, 2, 3)),
            dma((ATOMS, 2, 3)),
            dma((1 + ATOMS, 2)),
            dma((1 + ATOMS, 2)),
        ],
        compiler_params=pltpu.CompilerParams(collective_id=0, has_side_effects=True, vmem_limit_bytes=VMEM_LIMIT),
        name="sinkhorn_step",
    )(right_dual_factors, observed_mass_snapshot, basis_atom_masses, mixing_coefficient_tags)


def solution(mesh):
    placed = (
        P(None, "slab", None, None),
        P("grp", None, "slab", None, None),
        P("grp", "slab", None, None),
        P("grp", None),
    )
    return jax.shard_map(
        local,
        mesh=mesh,
        in_specs=placed,
        out_specs=(
            P("grp", "slab", None, None),
            P("grp", None, "slab", None, None),
            P(None, "grp", "slab", None),
        ),
        check_vma=False,
    )
```

```python
import math

import jax
import jax.numpy as jnp
import ml_dtypes
import numpy as np
from jax import lax
from jax.experimental import pallas as pl
from jax.experimental.pallas import tpu as pltpu
from jax.sharding import PartitionSpec as P

REACH = 4
SHARPNESS = 3.0
ATOMS = 3
ROWS = 16
NY = 128
NZ = 128
HALF = 8
MESH = pl.DeviceIdType.MESH
f32 = jnp.float32
bf16 = jnp.bfloat16
LN2 = math.log(2.0)
CODE_TOP = 32760.0
VMEM_LIMIT = 61184 * 2**10

TAPS = [math.exp(-SHARPNESS * (d / REACH) ** 2) / (REACH * math.sqrt(math.pi / SHARPNESS)) for d in range(REACH + 1)]

V_LOW, V_HIGH = math.log(0.0295), math.log(34.6)
F_LOW, F_HIGH = math.log(8.0e-4), math.log(5.2e3)


def code_of(low, high):
    scale = 65532.0 / (high - low)
    return scale, -32766.0 - low * scale


V_CODE = code_of(V_LOW, V_HIGH)
F_CODE = code_of(F_LOW, F_HIGH)


def encode(values, code):
    scale, shift = code
    return jnp.floor(jnp.log(values) * scale + (shift + 0.5)).astype(jnp.int32).astype(jnp.int16)


def decode(codes, code):
    scale, shift = code
    return jnp.exp(codes.astype(jnp.int32).astype(f32) * (1.0 / scale) - shift / scale)


HIGH = [float(np.float32(t).astype(ml_dtypes.bfloat16)) for t in TAPS]
LOW = [float((np.float32(t) - np.float32(h)).astype(ml_dtypes.bfloat16)) for t, h in zip(TAPS, HIGH)]


def band(taps, n):
    offset = jnp.abs(lax.broadcasted_iota(jnp.int32, (n, n), 0) - lax.broadcasted_iota(jnp.int32, (n, n), 1))
    g = jnp.zeros((n, n), f32)
    for d, tap in enumerate(taps):
        g = jnp.where(offset == d, tap, g)
    return g.astype(bf16)


def parts(x):
    high = x.astype(bf16)
    return high, (x - high.astype(f32)).astype(bf16)


def kernel(
    v_hbm, b_hbm, p_hbm, tags,
    bary, scal, gout,
    gz, gy, vbuf, fbuf, rk, lk, bbuf, pbuf,
    s1, s2, s3, r1, r2, r3,
    gsend, crecv, ysum, ycode, yrecv, fsize, fsend0, fsend1, frecv0, frecv1,
    in_sem, h_send, h_recv, c_send, c_recv, y_send, y_recv, f_send, f_recv,
):
    g = lax.axis_index("grp")
    s = lax.axis_index("slab")
    y, lo, c = g // 4, (g // 2) % 2, g % 2
    left = (g, (s + 15) % 16)
    right = (g, (s + 1) % 16)
    twin = (y * 4 + lo * 2 + (1 - c), s)

    def across_y(d):
        return (((y + d) % 4) * 4 + lo * 2 + c, s)

    z = s // 2
    pair = (y + 2 * c) % 4

    def ahead(k, i):
        return (z + k + 4 * i) % 8

    def owner(i):
        return (s, 2 * ahead(pair, i) + 1 - c)

    giver_core = 1 - s % 2
    giver_y = ((s // 2 - g // 2 + 8) % 8 + 4 - 2 * giver_core) % 4

    def giver(l):
        return (giver_y * 4 + l * 2 + giver_core, g)

    v_in = [pltpu.make_async_copy(v_hbm.at[0, a], vbuf.at[a, pl.ds(REACH, ROWS)], in_sem.at[a]) for a in range(ATOMS)]
    p_in = pltpu.make_async_copy(p_hbm, pbuf, in_sem.at[3])
    b_in = pltpu.make_async_copy(b_hbm.at[0], bbuf, in_sem.at[4])
    for copy in v_in + [p_in, b_in]:
        copy.start()

    barrier = pltpu.get_barrier_semaphore()
    peers = [left, right, twin] + [across_y(d) for d in (1, 2, 3)] + [owner(0), owner(1), giver(0), giver(1)]
    for peer in peers:
        pl.semaphore_signal(barrier, inc=1, device_id=peer, device_id_type=MESH)

    high, low, zero = band(HIGH, NZ), band(LOW, NZ), jnp.zeros((NZ, NZ), bf16)
    gz[...] = jnp.concatenate([jnp.concatenate([high, low], 1), jnp.concatenate([high, zero], 1)], 0)
    gy[...] = jnp.concatenate([jnp.concatenate([high, high], 1), jnp.concatenate([low, zero], 1)], 0)

    has_left = (s > 0).astype(f32)
    has_right = (s < 15).astype(f32)

    def remote(src, dst, send, recv, device):
        return pltpu.make_async_remote_copy(src_ref=src, dst_ref=dst, send_sem=send, recv_sem=recv, device_id=device, device_id_type=MESH)

    def halo(stage, a, q):
        src, dst = ((s1, r1), (s2, r2), (s3, r3))[stage]
        return remote(
            src.at[a, pl.ds(4 * q, 4)], dst.at[a, q], h_send.at[stage, a, q], h_recv.at[stage, a, q], (right, left)[q]
        )

    def halos(stage, a):
        return [halo(stage, a, q) for q in range(2)]

    def blur(buf, a, r):
        x = TAPS[0] * buf[a, r + REACH]
        for d in range(1, REACH + 1):
            x = x + TAPS[d] * (buf[a, r + REACH - d] + buf[a, r + REACH + d])
        high, low = parts(x)
        t = jnp.dot(jnp.concatenate([high, low], 1), gz[...], preferred_element_type=f32)
        high, low = parts(t[:, :NZ] + t[:, NZ:])
        t = jnp.dot(gy[...], jnp.concatenate([high, low], 0), preferred_element_type=f32)
        return t[:NY] + t[NY:]

    def row(part, i):
        return (4 + i) if part == 0 else (12 + i) % 16

    for a in range(ATOMS):
        v_in[a].wait()

        @pl.loop(0, HALF, unroll=2)
        def _(i):
            s1[a, i] = encode(vbuf[a, row(1, i) + REACH], V_CODE)

        if a == 0:
            pl.semaphore_wait(barrier, len(peers))
        for copy in halos(0, a):
            copy.start()

    p_in.wait()

    def span(side):
        return (0, HALF) if side is None else (4 * side, 4 * side + 4)

    def first(a, part):
        @pl.loop(0, HALF, unroll=8 if part else 4)
        def _(i):
            r = row(part, i)
            k = 1.0 / blur(vbuf, a, r)
            rk[a, r] = k
            f = pbuf[a, r].astype(f32) * k
            fbuf[a, r + REACH] = f
            if part == 1:
                s2[a, i] = encode(f, F_CODE)

    def second(a, part, side=None):
        @pl.loop(*span(side), unroll=8 if part and side is None else 4)
        def _(i):
            r = row(part, i)
            lk[a, r] = jnp.log(blur(fbuf, a, r))

    def land(stage, a, buf, side=None):
        sides = (0, 1) if side is None else (side,)
        for q in sides:
            halo(stage, a, 1 - q).wait_recv()
        dst = (r1, r2, r3)[stage]

        def value(x):
            return x.astype(f32) if stage == 2 else decode(x, (V_CODE, F_CODE)[stage])

        @pl.loop(0, 4, unroll=4)
        def _(i):
            if 1 in sides:
                buf[a, i] = value(dst[a, 0, i]) * has_left
            if 0 in sides:
                buf[a, i + REACH + ROWS] = value(dst[a, 1, i]) * has_right

    for a in range(ATOMS):
        first(a, 0)
    for a in range(ATOMS):
        land(0, a, vbuf)
        first(a, 1)
        for copy in halos(1, a):
            copy.start()
        second(a, 0)

    total = jnp.zeros((8, NZ), f32)
    weights = []
    for a in range(ATOMS):
        weights.append(jnp.full((8, NZ), tags[0, a], jnp.int32).astype(f32))
        total = total + weights[a]
    blend = [(w / total)[:1] for w in weights]

    def middle(part, side=None):
        @pl.loop(*span(side), unroll=2)
        def _(i):
            r = row(part, i)
            logs = [lk[a, r] for a in range(ATOMS)]
            mean = blend[0] * logs[0] + blend[1] * logs[1] + blend[2] * logs[2]
            center = jnp.exp(mean)
            bary[0, r] = center
            miss = center - bbuf[r]
            for a in range(ATOMS):
                ratio = jnp.exp(mean - logs[a])
                scal[0, a, r] = ratio
                pulled = blend[a] * miss * ratio
                vbuf[a, r + REACH] = pulled
                if part == 1:
                    s3[a, i] = pulled.astype(bf16)

    b_in.wait()
    middle(0)
    land(1, 0, fbuf)
    second(0, 1)
    land(1, 1, fbuf)
    second(1, 1)
    for side in range(2):
        land(1, 2, fbuf, side)
        second(2, 1, side)
        middle(1, side)
        for a in range(ATOMS):
            halo(2, a, side).start()

    def to_twin(a, part):
        return remote(gsend.at[a, part, c], crecv.at[a, part], c_send.at[a, part], c_recv.at[a, part], twin)

    def to_y(a, part, d):
        return remote(
            ycode.at[a, part, (pair + d) % 4], yrecv.at[a, part, d - 1], y_send.at[a, part, d - 1], y_recv.at[a, part, d - 1], across_y(d)
        )

    def to_owner(a, part, i):
        if part == 0:
            src, dst, n = fsend0.at[i], frecv0.at[lo], 0
        else:
            src, dst, n = fsend1.at[a, i], frecv1.at[a, lo], 1 + a
        return remote(src, dst, f_send.at[n, i], f_recv.at[n, lo], owner(i))

    def from_giver(a, part, l):
        if part == 0:
            src, dst, n = fsend0.at[0], frecv0.at[l], 0
        else:
            src, dst, n = fsend1.at[a, 0], frecv1.at[a, l], 1 + a
        return remote(src, dst, f_send.at[n, 0], f_recv.at[n, l], owner(0))

    def pack(t):
        top = jnp.maximum(jnp.max(jnp.abs(t), axis=0), 1e-30)
        size = jnp.ceil(jnp.log(top) * (16.0 / LN2))
        code = jnp.floor(t * (CODE_TOP * jnp.exp(size * (-LN2 / 16.0)))[None] + 0.5)
        return code.reshape(64, NZ).astype(jnp.int32).astype(jnp.int16), size

    def narrow(size):
        return size.astype(jnp.int32).astype(jnp.int16)

    def units(size):
        return jnp.exp(size.astype(jnp.int32).astype(f32) * (LN2 / 16.0)) * (1.0 / CODE_TOP)

    def unpack(code, unit):
        return code.astype(jnp.int32).astype(f32).reshape(HALF, 8, NZ) * unit[None]

    def third(a, part):
        @pl.loop(0, HALF, unroll=8 if part else 4)
        def _(i):
            r = row(part, i)
            t = (blur(vbuf, a, r) * rk[a, r]).reshape(8, 2, 8, NZ)
            gsend[a, part, 0, :, i] = t[:, 0]
            gsend[a, part, 1, :, i] = t[:, 1]

        to_twin(a, part).start()

    def over_cores(a, part):
        to_twin(a, part).wait_recv()

        @pl.loop(0, 4, unroll=4)
        def _(k):
            sizes = []
            for i in range(2):
                j = ahead(k, i)
                t = gsend[a, part, 1 - c, j] + crecv[a, part, j]
                ysum[a, part, k, i] = t
                ycode[a, part, k, pl.ds(64 * i, 64)], size = pack(t)
                sizes.append(size)
            ycode[a, part, k, pl.ds(128, 16)] = narrow(jnp.concatenate(sizes, 0))

        for d in (2, 1, 3):
            to_y(a, part, d).start()

    def over_y(a, part):
        for d in (1, 3, 2):
            to_y(a, part, d).wait_recv()
        scales = [units(yrecv[a, part, d, pl.ds(128, 16)]) for d in range(3)]
        for i in range(2):
            t = ysum[a, part, pair, i]
            for d in range(3):
                t = t + unpack(yrecv[a, part, d, pl.ds(64 * i, 64)], scales[d][8 * i : 8 * i + 8])
            code, size = pack(t)
            if part == 0:
                fsend0[i, pl.ds(64 * a, 64)] = code
                fsize[a, i] = size
                if a == ATOMS - 1:
                    sizes = jnp.concatenate([fsize[0, i], fsize[1, i], size, size], 0)
                    fsend0[i, pl.ds(192, 32)] = narrow(sizes)
                    to_owner(a, part, i).start()
            else:
                fsend1[a, i, pl.ds(0, 64)] = code
                fsend1[a, i, pl.ds(64, 16)] = narrow(jnp.concatenate([size, size], 0))
                to_owner(a, part, i).start()

    for a in range(ATOMS):
        third(a, 0)
    for a in range(ATOMS):
        over_cores(a, 0)
    land(2, 0, vbuf)
    third(0, 1)
    for a in range(ATOMS):
        over_y(a, 0)
    over_cores(0, 1)
    land(2, 1, vbuf)
    third(1, 1)
    over_y(0, 1)
    over_cores(1, 1)
    land(2, 2, vbuf)
    third(2, 1)
    over_cores(2, 1)
    over_y(1, 1)
    over_y(2, 1)

    for l in range(2):
        from_giver(0, 0, l).wait_recv()
    scales = [units(frecv0[l, pl.ds(192, 32)]) for l in range(2)]
    for a in range(ATOMS):
        t = [unpack(frecv0[l, pl.ds(64 * a, 64)], scales[l][8 * a : 8 * a + 8]) for l in range(2)]
        gout[a, pl.ds(4, 8)] = t[0] + t[1]
    for a in range(ATOMS):
        for l in range(2):
            from_giver(a, 1, l).wait_recv()
        t = [unpack(frecv1[a, l, pl.ds(0, 64)], units(frecv1[a, l, pl.ds(64, 16)])[:8]) for l in range(2)]
        t = t[0] + t[1]
        gout[a, pl.ds(12, 4)] = t[:4]
        gout[a, pl.ds(0, 4)] = t[4:]

    for a in range(ATOMS):
        for stage in range(3):
            for copy in halos(stage, a):
                copy.wait_send()
        for part in range(2):
            to_twin(a, part).wait_send()
            for d in (1, 2, 3):
                to_y(a, part, d).wait_send()
            for i in range(2 if part or a == 0 else 0):
                to_owner(a, part, i).wait_send()


def local(basis_atom_masses, right_dual_factors, observed_mass_snapshot, mixing_coefficient_tags):
    plane = (NY, NZ)
    vmem = pltpu.VMEM
    dma = pltpu.SemaphoreType.DMA
    outside = pl.BlockSpec(memory_space=pltpu.HBM)
    return pl.pallas_call(
        kernel,
        out_shape=(
            vmem((1, ROWS) + plane, f32),
            vmem((1, ATOMS, ROWS) + plane, f32),
            vmem((ATOMS, ROWS, 8, NZ), f32),
        ),
        in_specs=[
            outside,
            outside,
            outside,
            pl.BlockSpec(memory_space=pltpu.SMEM),
        ],
        out_specs=(pl.BlockSpec(memory_space=vmem),) * 3,
        scratch_shapes=[
            vmem((2 * NZ, 2 * NZ), bf16),
            vmem((2 * NY, 2 * NY), bf16),
            vmem((ATOMS, ROWS + 2 * REACH) + plane, f32),
            vmem((ATOMS, ROWS + 2 * REACH) + plane, f32),
            vmem((ATOMS, ROWS) + plane, f32),
            vmem((ATOMS, ROWS) + plane, f32),
            vmem((ROWS,) + plane, f32),
            vmem((ATOMS, ROWS) + plane, bf16),
            vmem((ATOMS, HALF) + plane, jnp.int16),
            vmem((ATOMS, HALF) + plane, jnp.int16),
            vmem((ATOMS, HALF) + plane, bf16),
            vmem((ATOMS, 2, 4) + plane, jnp.int16),
            vmem((ATOMS, 2, 4) + plane, jnp.int16),
            vmem((ATOMS, 2, 4) + plane, bf16),
            vmem((ATOMS, 2, 2, 8, HALF, 8, NZ), f32),
            vmem((ATOMS, 2, 8, HALF, 8, NZ), f32),
            vmem((ATOMS, 2, 4, 2, HALF, 8, NZ), f32),
            vmem((ATOMS, 2, 4, 144, NZ), jnp.int16),
            vmem((ATOMS, 2, 3, 144, NZ), jnp.int16),
            vmem((ATOMS, 2, 8, NZ), f32),
            vmem((2, 224, NZ), jnp.int16),
            vmem((ATOMS, 2, 80, NZ), jnp.int16),
            vmem((2, 224, NZ), jnp.int16),
            vmem((ATOMS, 2, 80, NZ), jnp.int16),
            dma((5,)),
            dma((3, ATOMS, 2)),
            dma((3, ATOMS, 2)),
            dma((ATOMS, 2)),
            dma((ATOMS, 2)),
            dma((ATOMS, 2, 3)),
            dma((ATOMS, 2, 3)),
            dma((1 + ATOMS, 2)),
            dma((1 + ATOMS, 2)),
        ],
        compiler_params=pltpu.CompilerParams(collective_id=0, has_side_effects=True, vmem_limit_bytes=VMEM_LIMIT),
        name="sinkhorn_step",
    )(right_dual_factors, observed_mass_snapshot, basis_atom_masses, mixing_coefficient_tags)


def solution(mesh):
    placed = (
        P(None, "slab", None, None),
        P("grp", None, "slab", None, None),
        P("grp", "slab", None, None),
        P("grp", None),
    )
    return jax.shard_map(
        local,
        mesh=mesh,
        in_specs=placed,
        out_specs=(
            P("grp", "slab", None, None),
            P("grp", None, "slab", None, None),
            P(None, "grp", "slab", None),
        ),
        check_vma=False,
    )
```

```python
import math

import jax
import jax.numpy as jnp
import ml_dtypes
import numpy as np
from jax import lax
from jax.experimental import pallas as pl
from jax.experimental.pallas import tpu as pltpu
from jax.sharding import PartitionSpec as P

REACH = 4
SHARPNESS = 3.0
ATOMS = 3
ROWS = 16
NY = 128
NZ = 128
HALF = 8
MESH = pl.DeviceIdType.MESH
f32 = jnp.float32
bf16 = jnp.bfloat16
LN2 = math.log(2.0)
CODE_TOP = 32760.0
VMEM_LIMIT = 61184 * 2**10

TAPS = [math.exp(-SHARPNESS * (d / REACH) ** 2) / (REACH * math.sqrt(math.pi / SHARPNESS)) for d in range(REACH + 1)]

V_LOW, V_HIGH = math.log(0.0295), math.log(34.6)
F_LOW, F_HIGH = math.log(8.0e-4), math.log(5.2e3)


def code_of(low, high):
    scale = 65532.0 / (high - low)
    return scale, -32766.0 - low * scale


V_CODE = code_of(V_LOW, V_HIGH)
F_CODE = code_of(F_LOW, F_HIGH)


def encode(values, code):
    scale, shift = code
    return jnp.floor(jnp.log(values) * scale + (shift + 0.5)).astype(jnp.int32).astype(jnp.int16)


def decode(codes, code):
    scale, shift = code
    return jnp.exp(codes.astype(jnp.int32).astype(f32) * (1.0 / scale) - shift / scale)


HIGH = [float(np.float32(t).astype(ml_dtypes.bfloat16)) for t in TAPS]
LOW = [float((np.float32(t) - np.float32(h)).astype(ml_dtypes.bfloat16)) for t, h in zip(TAPS, HIGH)]


def band(taps, n):
    offset = jnp.abs(lax.broadcasted_iota(jnp.int32, (n, n), 0) - lax.broadcasted_iota(jnp.int32, (n, n), 1))
    g = jnp.zeros((n, n), f32)
    for d, tap in enumerate(taps):
        g = jnp.where(offset == d, tap, g)
    return g.astype(bf16)


def parts(x):
    high = x.astype(bf16)
    return high, (x - high.astype(f32)).astype(bf16)


def kernel(
    v_hbm, b_hbm, p_hbm, tags,
    bary, scal, gout,
    gz, gy, vbuf, fbuf, rk, lk, bbuf, pbuf,
    s1, s2, s3, r1, r2, r3,
    gsend, crecv, ysum, ycode, yrecv, fsize, fsend0, fsend1, frecv0, frecv1,
    in_sem, h_send, h_recv, c_send, c_recv, y_send, y_recv, f_send, f_recv,
):
    g = lax.axis_index("grp")
    s = lax.axis_index("slab")
    y, lo, c = g // 4, (g // 2) % 2, g % 2
    left = (g, (s + 15) % 16)
    right = (g, (s + 1) % 16)
    twin = (y * 4 + lo * 2 + (1 - c), s)

    def across_y(d):
        return (((y + d) % 4) * 4 + lo * 2 + c, s)

    z = s // 2
    pair = (y + 2 * c) % 4

    def ahead(k, i):
        return (z + k + 4 * i) % 8

    def owner(i):
        return (s, 2 * ahead(pair, i) + 1 - c)

    giver_core = 1 - s % 2
    giver_y = ((s // 2 - g // 2 + 8) % 8 + 4 - 2 * giver_core) % 4

    def giver(l):
        return (giver_y * 4 + l * 2 + giver_core, g)

    v_in = [pltpu.make_async_copy(v_hbm.at[0, a], vbuf.at[a, pl.ds(REACH, ROWS)], in_sem.at[a]) for a in range(ATOMS)]
    p_in = pltpu.make_async_copy(p_hbm, pbuf, in_sem.at[3])
    b_in = pltpu.make_async_copy(b_hbm.at[0], bbuf, in_sem.at[4])
    for copy in v_in + [p_in, b_in]:
        copy.start()

    barrier = pltpu.get_barrier_semaphore()
    peers = [left, right, twin] + [across_y(d) for d in (1, 2, 3)] + [owner(0), owner(1), giver(0), giver(1)]
    for peer in peers:
        pl.semaphore_signal(barrier, inc=1, device_id=peer, device_id_type=MESH)

    high, low, zero = band(HIGH, NZ), band(LOW, NZ), jnp.zeros((NZ, NZ), bf16)
    gz[...] = jnp.concatenate([jnp.concatenate([high, low], 1), jnp.concatenate([high, zero], 1)], 0)
    gy[...] = jnp.concatenate([jnp.concatenate([high, high], 1), jnp.concatenate([low, zero], 1)], 0)

    has_left = (s > 0).astype(f32)
    has_right = (s < 15).astype(f32)

    def remote(src, dst, send, recv, device):
        return pltpu.make_async_remote_copy(src_ref=src, dst_ref=dst, send_sem=send, recv_sem=recv, device_id=device, device_id_type=MESH)

    def halo(stage, a, q):
        src, dst = ((s1, r1), (s2, r2), (s3, r3))[stage]
        return remote(
            src.at[a, pl.ds(4 * q, 4)], dst.at[a, q], h_send.at[stage, a, q], h_recv.at[stage, a, q], (right, left)[q]
        )

    def halos(stage, a):
        return [halo(stage, a, q) for q in range(2)]

    def blur(buf, a, r):
        x = TAPS[0] * buf[a, r + REACH]
        for d in range(1, REACH + 1):
            x = x + TAPS[d] * (buf[a, r + REACH - d] + buf[a, r + REACH + d])
        high, low = parts(x)
        t = jnp.dot(jnp.concatenate([high, low], 1), gz[...], preferred_element_type=f32)
        high, low = parts(t[:, :NZ] + t[:, NZ:])
        t = jnp.dot(gy[...], jnp.concatenate([high, low], 0), preferred_element_type=f32)
        return t[:NY] + t[NY:]

    def row(part, i):
        return (4 + i) if part == 0 else (12 + i) % 16

    for a in range(ATOMS):
        v_in[a].wait()

        @pl.loop(0, HALF, unroll=2)
        def _(i):
            s1[a, i] = encode(vbuf[a, row(1, i) + REACH], V_CODE)

        if a == 0:
            pl.semaphore_wait(barrier, len(peers))
        for copy in halos(0, a):
            copy.start()

    p_in.wait()

    def span(side):
        return (0, HALF) if side is None else (4 * side, 4 * side + 4)

    def first(a, part):
        @pl.loop(0, HALF, unroll=8 if part else 4)
        def _(i):
            r = row(part, i)
            k = 1.0 / blur(vbuf, a, r)
            rk[a, r] = k
            f = pbuf[a, r].astype(f32) * k
            fbuf[a, r + REACH] = f
            if part == 1:
                s2[a, i] = encode(f, F_CODE)

    def second(a, part, side=None):
        @pl.loop(*span(side), unroll=8 if part and side is None else 4)
        def _(i):
            r = row(part, i)
            lk[a, r] = jnp.log(blur(fbuf, a, r))

    def land(stage, a, buf, side=None):
        sides = (0, 1) if side is None else (side,)
        for q in sides:
            halo(stage, a, 1 - q).wait_recv()
        dst = (r1, r2, r3)[stage]

        def value(x):
            return x.astype(f32) if stage == 2 else decode(x, (V_CODE, F_CODE)[stage])

        @pl.loop(0, 4, unroll=4)
        def _(i):
            if 1 in sides:
                buf[a, i] = value(dst[a, 0, i]) * has_left
            if 0 in sides:
                buf[a, i + REACH + ROWS] = value(dst[a, 1, i]) * has_right

    for a in range(ATOMS):
        first(a, 0)
    for a in range(ATOMS):
        land(0, a, vbuf)
        first(a, 1)
        for copy in halos(1, a):
            copy.start()
        second(a, 0)

    total = jnp.zeros((8, NZ), f32)
    weights = []
    for a in range(ATOMS):
        weights.append(jnp.full((8, NZ), tags[0, a], jnp.int32).astype(f32))
        total = total + weights[a]
    blend = [(w / total)[:1] for w in weights]

    def middle(part, side=None):
        @pl.loop(*span(side), unroll=2)
        def _(i):
            r = row(part, i)
            logs = [lk[a, r] for a in range(ATOMS)]
            mean = blend[0] * logs[0] + blend[1] * logs[1] + blend[2] * logs[2]
            center = jnp.exp(mean)
            bary[0, r] = center
            miss = center - bbuf[r]
            for a in range(ATOMS):
                ratio = jnp.exp(mean - logs[a])
                scal[0, a, r] = ratio
                pulled = blend[a] * miss * ratio
                vbuf[a, r + REACH] = pulled
                if part == 1:
                    s3[a, i] = pulled.astype(bf16)

    b_in.wait()
    middle(0)
    land(1, 0, fbuf)
    second(0, 1)
    land(1, 1, fbuf)
    second(1, 1)
    for side in range(2):
        land(1, 2, fbuf, side)
        second(2, 1, side)
        middle(1, side)
        for a in range(ATOMS):
            halo(2, a, side).start()

    def to_twin(a, part):
        return remote(gsend.at[a, part, c], crecv.at[a, part], c_send.at[a, part], c_recv.at[a, part], twin)

    def to_y(a, part, d):
        return remote(
            ycode.at[a, part, (pair + d) % 4], yrecv.at[a, part, d - 1], y_send.at[a, part, d - 1], y_recv.at[a, part, d - 1], across_y(d)
        )

    def to_owner(a, part, i):
        if part == 0:
            src, dst, n = fsend0.at[i], frecv0.at[lo], 0
        else:
            src, dst, n = fsend1.at[a, i], frecv1.at[a, lo], 1 + a
        return remote(src, dst, f_send.at[n, i], f_recv.at[n, lo], owner(i))

    def from_giver(a, part, l):
        if part == 0:
            src, dst, n = fsend0.at[0], frecv0.at[l], 0
        else:
            src, dst, n = fsend1.at[a, 0], frecv1.at[a, l], 1 + a
        return remote(src, dst, f_send.at[n, 0], f_recv.at[n, l], owner(0))

    def pack(t):
        top = jnp.maximum(jnp.max(jnp.abs(t), axis=0), 1e-30)
        size = jnp.ceil(jnp.log(top) * (16.0 / LN2))
        code = jnp.floor(t * (CODE_TOP * jnp.exp(size * (-LN2 / 16.0)))[None] + 0.5)
        return code.reshape(64, NZ).astype(jnp.int32).astype(jnp.int16), size

    def narrow(size):
        return size.astype(jnp.int32).astype(jnp.int16)

    def units(size):
        return jnp.exp(size.astype(jnp.int32).astype(f32) * (LN2 / 16.0)) * (1.0 / CODE_TOP)

    def unpack(code, unit):
        return code.astype(jnp.int32).astype(f32).reshape(HALF, 8, NZ) * unit[None]

    def third(a, part):
        @pl.loop(0, HALF, unroll=8 if part else 4)
        def _(i):
            r = row(part, i)
            t = (blur(vbuf, a, r) * rk[a, r]).reshape(8, 2, 8, NZ)
            gsend[a, part, 0, :, i] = t[:, 0]
            gsend[a, part, 1, :, i] = t[:, 1]

        to_twin(a, part).start()

    def over_cores(a, part):
        to_twin(a, part).wait_recv()

        @pl.loop(0, 4, unroll=4)
        def _(k):
            sizes = []
            for i in range(2):
                j = ahead(k, i)
                t = gsend[a, part, 1 - c, j] + crecv[a, part, j]
                ysum[a, part, k, i] = t
                ycode[a, part, k, pl.ds(64 * i, 64)], size = pack(t)
                sizes.append(size)
            ycode[a, part, k, pl.ds(128, 16)] = narrow(jnp.concatenate(sizes, 0))

        for d in (2, 1, 3):
            to_y(a, part, d).start()

    def over_y(a, part):
        for d in (1, 3, 2):
            to_y(a, part, d).wait_recv()
        scales = [units(yrecv[a, part, d, pl.ds(128, 16)]) for d in range(3)]
        for i in range(2):
            t = ysum[a, part, pair, i]
            for d in range(3):
                t = t + unpack(yrecv[a, part, d, pl.ds(64 * i, 64)], scales[d][8 * i : 8 * i + 8])
            code, size = pack(t)
            if part == 0:
                fsend0[i, pl.ds(64 * a, 64)] = code
                fsize[a, i] = size
                if a == ATOMS - 1:
                    sizes = jnp.concatenate([fsize[0, i], fsize[1, i], size, size], 0)
                    fsend0[i, pl.ds(192, 32)] = narrow(sizes)
                    to_owner(a, part, i).start()
            else:
                fsend1[a, i, pl.ds(0, 64)] = code
                fsend1[a, i, pl.ds(64, 16)] = narrow(jnp.concatenate([size, size], 0))
                to_owner(a, part, i).start()

    for a in range(ATOMS):
        third(a, 0)
    for a in range(ATOMS):
        over_cores(a, 0)
    land(2, 0, vbuf)
    third(0, 1)
    for a in range(ATOMS):
        over_y(a, 0)
    over_cores(0, 1)
    land(2, 1, vbuf)
    third(1, 1)
    over_cores(1, 1)
    over_y(0, 1)
    land(2, 2, vbuf)
    third(2, 1)
    over_cores(2, 1)
    over_y(1, 1)
    over_y(2, 1)

    for l in range(2):
        from_giver(0, 0, l).wait_recv()
    scales = [units(frecv0[l, pl.ds(192, 32)]) for l in range(2)]
    for a in range(ATOMS):
        t = [unpack(frecv0[l, pl.ds(64 * a, 64)], scales[l][8 * a : 8 * a + 8]) for l in range(2)]
        gout[a, pl.ds(4, 8)] = t[0] + t[1]
    for a in range(ATOMS):
        for l in range(2):
            from_giver(a, 1, l).wait_recv()
        t = [unpack(frecv1[a, l, pl.ds(0, 64)], units(frecv1[a, l, pl.ds(64, 16)])[:8]) for l in range(2)]
        t = t[0] + t[1]
        gout[a, pl.ds(12, 4)] = t[:4]
        gout[a, pl.ds(0, 4)] = t[4:]

    for a in range(ATOMS):
        for stage in range(3):
            for copy in halos(stage, a):
                copy.wait_send()
        for part in range(2):
            to_twin(a, part).wait_send()
            for d in (1, 2, 3):
                to_y(a, part, d).wait_send()
            for i in range(2 if part or a == 0 else 0):
                to_owner(a, part, i).wait_send()


def local(basis_atom_masses, right_dual_factors, observed_mass_snapshot, mixing_coefficient_tags):
    plane = (NY, NZ)
    vmem = pltpu.VMEM
    dma = pltpu.SemaphoreType.DMA
    outside = pl.BlockSpec(memory_space=pltpu.HBM)
    return pl.pallas_call(
        kernel,
        out_shape=(
            vmem((1, ROWS) + plane, f32),
            vmem((1, ATOMS, ROWS) + plane, f32),
            vmem((ATOMS, ROWS, 8, NZ), f32),
        ),
        in_specs=[
            outside,
            outside,
            outside,
            pl.BlockSpec(memory_space=pltpu.SMEM),
        ],
        out_specs=(pl.BlockSpec(memory_space=vmem),) * 3,
        scratch_shapes=[
            vmem((2 * NZ, 2 * NZ), bf16),
            vmem((2 * NY, 2 * NY), bf16),
            vmem((ATOMS, ROWS + 2 * REACH) + plane, f32),
            vmem((ATOMS, ROWS + 2 * REACH) + plane, f32),
            vmem((ATOMS, ROWS) + plane, f32),
            vmem((ATOMS, ROWS) + plane, f32),
            vmem((ROWS,) + plane, f32),
            vmem((ATOMS, ROWS) + plane, bf16),
            vmem((ATOMS, HALF) + plane, jnp.int16),
            vmem((ATOMS, HALF) + plane, jnp.int16),
            vmem((ATOMS, HALF) + plane, bf16),
            vmem((ATOMS, 2, 4) + plane, jnp.int16),
            vmem((ATOMS, 2, 4) + plane, jnp.int16),
            vmem((ATOMS, 2, 4) + plane, bf16),
            vmem((ATOMS, 2, 2, 8, HALF, 8, NZ), f32),
            vmem((ATOMS, 2, 8, HALF, 8, NZ), f32),
            vmem((ATOMS, 2, 4, 2, HALF, 8, NZ), f32),
            vmem((ATOMS, 2, 4, 144, NZ), jnp.int16),
            vmem((ATOMS, 2, 3, 144, NZ), jnp.int16),
            vmem((ATOMS, 2, 8, NZ), f32),
            vmem((2, 224, NZ), jnp.int16),
            vmem((ATOMS, 2, 80, NZ), jnp.int16),
            vmem((2, 224, NZ), jnp.int16),
            vmem((ATOMS, 2, 80, NZ), jnp.int16),
            dma((5,)),
            dma((3, ATOMS, 2)),
            dma((3, ATOMS, 2)),
            dma((ATOMS, 2)),
            dma((ATOMS, 2)),
            dma((ATOMS, 2, 3)),
            dma((ATOMS, 2, 3)),
            dma((1 + ATOMS, 2)),
            dma((1 + ATOMS, 2)),
        ],
        compiler_params=pltpu.CompilerParams(collective_id=0, has_side_effects=True, vmem_limit_bytes=VMEM_LIMIT),
        name="sinkhorn_step",
    )(right_dual_factors, observed_mass_snapshot, basis_atom_masses, mixing_coefficient_tags)


def solution(mesh):
    placed = (
        P(None, "slab", None, None),
        P("grp", None, "slab", None, None),
        P("grp", "slab", None, None),
        P("grp", None),
    )
    return jax.shard_map(
        local,
        mesh=mesh,
        in_specs=placed,
        out_specs=(
            P("grp", "slab", None, None),
            P("grp", None, "slab", None, None),
            P(None, "grp", "slab", None),
        ),
        check_vma=False,
    )
```
